32 devices in a mesh: ex: 4 (over x, core), ft: 8 (over z, y).
Axes of the slice: x: 2, y: 2, z: 4, core: 2. Of those that a mesh axis runs over, the one named last changes fastest.
Arguments:
- features: bfloat16 [32768, 16384], P('ex', 'ft'), as said below
- targets: float32 [8, 32768], P(None, 'ex'), may hold values from -36 to 36, as said below
Outputs:
- estimate: float32 [8, 16384], P(None, 'ft')
- misfit: float32 [8, 32768], P(None, 'ex')
The draws below stay inside these ranges and needn't reach their ends.
Inputs may be any that keep to these rules, and one draw needn't show every extreme that they name: Finite; row and column scales vary over examples and features. `targets`: Finite.
All inputs are finite; a program needn't handle non-finite values.
Results may differ from the reference program's by a relative error of at most 0.0034.
Values sent between devices are 32-bit elements; how exact they have to be, the bound alone decides.
A program may use at most 64 MiB of HBM per device.

```python
import math
import jax
import jax.numpy as jnp
from jax import lax

FEATURES = 16384
TESTS = 8
ITERS = 2
EXAMPLES = 32768


def draw_features(key, part):
    key = jax.random.fold_in(key, 11)
    noise_key, row_key, col_key = jax.random.split(key, 3)
    noise = jnp.clip(jax.random.normal(noise_key, (EXAMPLES, FEATURES), jnp.float32), -6.0, 6.0)
    row_pos = jnp.arange(EXAMPLES, dtype=jnp.float32) / EXAMPLES
    col_pos = jnp.arange(FEATURES, dtype=jnp.float32) / FEATURES
    row_scale = jnp.exp(jax.random.uniform(row_key, (EXAMPLES,), jnp.float32, math.log(0.5), math.log(5.0)) + math.log(3.0) * row_pos) / 2.0
    col_scale = jnp.exp(jax.random.uniform(col_key, (FEATURES,), jnp.float32, math.log(0.5), math.log(5.0)) + math.log(3.0) * col_pos) / 2.0
    values = noise * row_scale[:, None] * col_scale[None, :] * (0.5 / math.sqrt(EXAMPLES))
    return values.astype(jnp.bfloat16)


def draw_targets(key, part):
    key = jax.random.fold_in(key, 23)
    noise_key, test_key = jax.random.split(key)
    noise = jnp.clip(jax.random.normal(noise_key, (TESTS, EXAMPLES), jnp.float32), -6.0, 6.0)
    row_pos = jnp.arange(EXAMPLES, dtype=jnp.float32) / EXAMPLES
    test_scale = jnp.exp(jax.random.uniform(test_key, (TESTS, 1), jnp.float32, math.log(0.5), math.log(2.0)))
    return noise * test_scale * jnp.exp(math.log(3.0) * row_pos)[None, :]


def setup_inputs(seed: int = 0) -> dict:
    key_list = jax.random.split(jax.random.key(seed), 3)
    return {
        "features": draw_features(jax.random.fold_in(key_list[2], 71), 0),
        "targets": draw_targets(jax.random.fold_in(key_list[2], 71), 0),
    }


eps = 1e-06

def row_norm(vector):
    return jnp.sqrt(lax.optimization_barrier(jnp.sum(vector * vector, axis=1, keepdims=True)) + eps)

def times_rows(right_vec, features):
    return lax.dot_general(right_vec.astype(jnp.bfloat16), features, (((1,), (1,)), ((), ())), preferred_element_type=jnp.float32)

def reference(features, targets):
    beta_norm = row_norm(targets)
    left_vec = targets / beta_norm
    right_pre = jnp.dot(left_vec.astype(jnp.bfloat16), features, preferred_element_type=jnp.float32)
    alpha_norm = row_norm(right_pre)
    right_vec = right_pre / alpha_norm
    search = right_vec
    estimate = jnp.zeros_like(right_vec)
    phi_bar = beta_norm
    rho_bar = alpha_norm
    for step in range(ITERS):
        left_pre = times_rows(right_vec, features) - alpha_norm * left_vec
        beta_norm = row_norm(left_pre)
        left_vec = left_pre / beta_norm
        right_pre = jnp.dot(left_vec.astype(jnp.bfloat16), features, preferred_element_type=jnp.float32) - beta_norm * right_vec
        alpha_norm = row_norm(right_pre)
        right_vec = right_pre / alpha_norm
        rho_value = jnp.sqrt(rho_bar * rho_bar + beta_norm * beta_norm)
        cosine = rho_bar / rho_value
        sine_value = beta_norm / rho_value
        theta_value = sine_value * alpha_norm
        rho_bar = -cosine * alpha_norm
        phi_value = cosine * phi_bar
        phi_bar = sine_value * phi_bar
        estimate = estimate + phi_value / rho_value * search
        search = right_vec - theta_value / rho_value * search
    misfit = targets - times_rows(estimate, features)
    return (estimate, misfit)
```

```python
import functools

import jax
import jax.numpy as jnp
from jax import lax
from jax.experimental import pallas as pl
from jax.experimental.pallas import tpu as pltpu
from jax.sharding import PartitionSpec as P

eps = 1e-06
F32 = jnp.float32
MESH = pl.DeviceIdType.MESH
NT = (((1,), (1,)), ((), ()))

BLOCKS = 4
CHUNKS = 4


def split16(x):
    hi = x.astype(jnp.bfloat16).astype(F32)
    return jnp.concatenate([hi, x - hi], axis=0).astype(jnp.bfloat16)


def fold(r):
    return r[:8] + r[8:]


def squares(x):
    return jnp.sum(x * x, axis=1, keepdims=True)


def kernel(
    n_ex, n_ft, a_ref, t_ref, est_ref, mis_ref,
    av, u16, w16, acc, pacc, rp, left, p0, p1, qs, rsb, ag, nx, nf,
    hbm, ssem, rsem,
):
    rows, cols = av.shape
    cb = cols // BLOCKS
    rc = rows // CHUNKS
    piece = rc // n_ft
    half = cols // 2
    ex, ft = lax.axis_index("ex"), lax.axis_index("ft")

    loads = []
    for j in range(BLOCKS):
        c = pl.ds(j * cb, cb)
        load = pltpu.make_async_copy(a_ref.at[:, c], av.at[:, c], hbm.at[j])
        load.start()
        loads.append(load)

    barrier = pltpu.get_barrier_semaphore()
    for axis, n, me in (("ex", n_ex, ex), ("ft", n_ft, ft)):
        @pl.loop(1, n)
        def _(d):
            pl.semaphore_signal(
                barrier, inc=1, device_id={axis: lax.rem(me + d, n)}, device_id_type=MESH
            )
    pl.semaphore_wait(barrier, n_ex + n_ft - 2)

    groups = {}

    def send(name, axis, src, dst, region):
        n, me = (n_ex, ex) if axis == "ex" else (n_ft, ft)
        g = len(groups)
        groups[name] = (g, region)

        @pl.loop(1, n)
        def _(d):
            peer = lax.rem(me + d, n)
            pltpu.make_async_remote_copy(
                src_ref=src(peer), dst_ref=dst, send_sem=ssem.at[g], recv_sem=rsem.at[g],
                device_id={axis: peer}, device_id_type=MESH,
            ).start()

    def arrive(name):
        g, region = groups[name]
        pltpu.make_async_copy(region, region, rsem.at[g]).wait()

    def put_norm(k, axis, square):
        buf, n, me = (nx, n_ex, ex) if axis == "ex" else (nf, n_ft, ft)
        buf[k, me] = jnp.broadcast_to(square, (8, 128))
        own = buf.at[k, me]
        send(("norm", axis, k), axis, lambda peer: own, own, buf.at[k, pl.ds(0, n - 1)])

    def get_norm(k, axis):
        buf, n = (nx, n_ex) if axis == "ex" else (nf, n_ft)
        arrive(("norm", axis, k))
        total = buf[k, 0]
        for i in range(1, n):
            total = total + buf[k, i]
        return jnp.sqrt(total + eps)[:, :1]

    def spread(buf, name, j, value):
        buf[j, ex] = value
        own = buf.at[j, ex]
        send((name, j), "ex", lambda peer: own, own, buf.at[j, pl.ds(0, n_ex - 1)])

    def gathered(buf, name, j):
        arrive((name, j))
        total = buf[j, 0]
        for i in range(1, n_ex):
            total = total + buf[j, i]
        return total

    def times_rows(c, first):
        @pl.loop(0, CHUNKS)
        def _(i):
            r = pl.ds(pl.multiple_of(i * rc, rc), rc)
            out = lax.dot_general(w16[:, c], av[r, c], NT, preferred_element_type=F32)
            acc[:, r] = out if first else acc[:, r] + out

    def rows_send(q, ch, c):
        r = pl.ds(ch * rc, rc)
        out = lax.dot_general(w16[:, c], av[r, c], NT, preferred_element_type=F32)
        out = fold(acc[:, r] + out)
        for i in range(n_ft):
            qs[q, ch, i] = out[:, i * piece:(i + 1) * piece]
        rsb[q, ch, ft] = qs[q, ch, ft]
        send(
            ("rs", q, ch), "ft", lambda peer: qs.at[q, ch, peer], rsb.at[q, ch, ft],
            rsb.at[q, ch, pl.ds(0, n_ft - 1)],
        )

    def rows_sum(q, ch):
        arrive(("rs", q, ch))
        total = rsb[q, ch, 0]
        for i in range(1, n_ft):
            total = total + rsb[q, ch, i]
        ag[q, ch, ft] = total
        own = ag.at[q, ch, ft]
        send(("ag", q, ch), "ft", lambda peer: own, own, ag.at[q, ch, pl.ds(0, n_ft - 1)])

    def rows_get(q, ch):
        arrive(("ag", q, ch))
        return jnp.concatenate([ag[q, ch, i] for i in range(n_ft)], axis=1)

    put_norm(0, "ex", squares(t_ref[...]))
    u16[...] = split16(t_ref[...])

    def first_columns(j):
        loads[j].wait()
        c = pl.ds(j * cb, cb)
        spread(p0, "p0", j, fold(jnp.dot(u16[...], av[:, c], preferred_element_type=F32)))

    first_columns(0)
    first_columns(1)
    beta0 = get_norm(0, "ex")
    left[...] = t_ref[...] / beta0
    square = jnp.zeros((8, 1), F32)
    for j in range(BLOCKS):
        c = pl.ds(j * cb, cb)
        fresh = gathered(p0, "p0", j) / beta0
        square = square + squares(fresh)
        rp[:, c] = fresh
        w16[:, c] = split16(fresh)
        if j == BLOCKS - 1:
            put_norm(0, "ft", square)
            break
        times_rows(c, j == 0)
        if j + 2 < BLOCKS:
            first_columns(j + 2)

    last = pl.ds((BLOCKS - 1) * cb, cb)
    for ch in range(CHUNKS):
        rows_send(0, ch, last)
        if ch >= 2:
            rows_sum(0, ch - 2)
    alpha0 = get_norm(0, "ft")

    square = jnp.zeros((8, 1), F32)
    for ch in range(CHUNKS):
        if ch + 2 < CHUNKS:
            rows_sum(0, ch + 2)
        r = pl.ds(ch * rc, rc)
        fresh = rows_get(0, ch) / alpha0 - alpha0 * left[:, r]
        square = square + squares(fresh)
        left[:, r] = fresh
        u16[:, r] = split16(fresh)
        if ch < CHUNKS - 1:
            out = jnp.dot(u16[:, r], av[r, :], preferred_element_type=F32)
            pacc[...] = out if ch == 0 else pacc[...] + out
        else:
            put_norm(1, "ex", square)
            for h in range(2):
                c = pl.ds(h * half, half)
                out = jnp.dot(u16[:, r], av[r, c], preferred_element_type=F32)
                spread(p1, "p1", h, fold(pacc[:, c] + out))
    beta1 = get_norm(1, "ex")

    square = jnp.zeros((8, 1), F32)
    for h in range(2):
        c = pl.ds(h * half, half)
        v0 = rp[:, c] / alpha0
        fresh = gathered(p1, "p1", h) / beta1 - beta1 * v0
        square = square + squares(fresh)
        rp[:, c] = v0
        est_ref[:, c] = fresh
        w16[:, c] = split16(fresh)
        if h == 0:
            times_rows(c, True)
    put_norm(1, "ft", square)
    last = pl.ds(half, half)
    for ch in range(CHUNKS):
        rows_send(1, ch, last)
        if ch >= 2:
            rows_sum(1, ch - 2)
    alpha1 = get_norm(1, "ft")
    square = jnp.zeros((8, 1), F32)
    for ch in range(CHUNKS):
        if ch + 2 < CHUNKS:
            rows_sum(1, ch + 2)
        r = pl.ds(ch * rc, rc)
        fitted = rows_get(1, ch) / alpha1
        mis_ref[:, r] = fitted
        square = square + squares(fitted - alpha1 * (left[:, r] / beta1))
    put_norm(2, "ex", square)
    beta2 = get_norm(2, "ex")

    rho = jnp.sqrt(alpha0 * alpha0 + beta1 * beta1)
    cosine = alpha0 / rho
    sine = beta1 / rho
    theta = sine * alpha1
    rho_bar = -cosine * alpha1
    step1 = cosine * beta0 / rho
    rho2 = jnp.sqrt(rho_bar * rho_bar + beta2 * beta2)
    step2 = rho_bar / rho2 * (sine * beta0) / rho2
    weight0 = step1 - step2 * (theta / rho)
    est_ref[...] = weight0 * rp[...] + step2 * (est_ref[...] / alpha1)
    scale0 = weight0 / alpha0
    for ch in range(CHUNKS):
        for i in range(n_ft):
            r = pl.ds(ch * rc + i * piece, piece)
            mis_ref[:, r] = t_ref[:, r] - (scale0 * ag[0, ch, i] + step2 * mis_ref[:, r])

    for g, region in groups.values():
        pltpu.make_async_copy(region, region, ssem.at[g]).wait()


def solution(mesh):
    n_ex, n_ft = mesh.shape["ex"], mesh.shape["ft"]

    def shards(features, targets):
        rows, cols = features.shape
        piece = rows // CHUNKS // n_ft
        n_groups = BLOCKS + 2 + 4 * CHUNKS + 5
        vmem = pltpu.VMEM
        return pl.pallas_call(
            functools.partial(kernel, n_ex, n_ft),
            out_shape=(
                jax.ShapeDtypeStruct((8, cols), F32),
                jax.ShapeDtypeStruct((8, rows), F32),
            ),
            in_specs=[pl.BlockSpec(memory_space=pl.ANY), pl.BlockSpec(memory_space=vmem)],
            out_specs=(pl.BlockSpec(memory_space=vmem), pl.BlockSpec(memory_space=vmem)),
            scratch_shapes=[
                vmem((rows, cols), jnp.bfloat16),
                vmem((16, rows), jnp.bfloat16),
                vmem((16, cols), jnp.bfloat16),
                vmem((16, rows), F32),
                vmem((16, cols), F32),
                vmem((8, cols), F32),
                vmem((8, rows), F32),
                vmem((BLOCKS, n_ex, 8, cols // BLOCKS), F32),
                vmem((2, n_ex, 8, cols // 2), F32),
                vmem((2, CHUNKS, n_ft, 8, piece), F32),
                vmem((2, CHUNKS, n_ft, 8, piece), F32),
                vmem((2, CHUNKS, n_ft, 8, piece), F32),
                vmem((3, n_ex, 8, 128), F32),
                vmem((2, n_ft, 8, 128), F32),
                pltpu.SemaphoreType.DMA((BLOCKS,)),
                pltpu.SemaphoreType.DMA((n_groups,)),
                pltpu.SemaphoreType.DMA((n_groups,)),
            ],
            compiler_params=pltpu.CompilerParams(
                collective_id=0, has_side_effects=True, vmem_limit_bytes=58 << 20
            ),
        )(features, targets)

    return jax.shard_map(
        shards,
        mesh=mesh,
        in_specs=(P("ex", "ft"), P(None, "ex")),
        out_specs=(P(None, "ft"), P(None, "ex")),
        check_vma=False,
    )
```

```python
import functools

import jax
import jax.numpy as jnp
from jax import lax
from jax.experimental import pallas as pl
from jax.experimental.pallas import tpu as pltpu
from jax.sharding import PartitionSpec as P

eps = 1e-06
F32 = jnp.float32
MESH = pl.DeviceIdType.MESH
NT = (((1,), (1,)), ((), ()))

BLOCKS = 4
CHUNKS = 4


def split16(x):
    hi = x.astype(jnp.bfloat16).astype(F32)
    return jnp.concatenate([hi, x - hi], axis=0).astype(jnp.bfloat16)


def fold(r):
    return r[:8] + r[8:]


def squares(x):
    return jnp.sum(x * x, axis=1, keepdims=True)


def kernel(
    n_ex, n_ft, n_in, a_ref, t_ref, est_ref, mis_ref,
    av, u16, w16, acc, pacc, rp, left, p0, p1, qs, r1, s1, r2, ag, nx, nf,
    hbm, ssem, rsem,
):
    rows, cols = av.shape
    cb = cols // BLOCKS
    rc = rows // CHUNKS
    piece = rc // n_ft
    half = cols // 2
    ex, ft = lax.axis_index("ex"), lax.axis_index("ft")
    n_out = n_ft // n_in
    outer, inner = ft // n_in, lax.rem(ft, n_in)

    loads = []
    for j in range(BLOCKS):
        c = pl.ds(j * cb, cb)
        load = pltpu.make_async_copy(a_ref.at[:, c], av.at[:, c], hbm.at[j])
        load.start()
        loads.append(load)

    barrier = pltpu.get_barrier_semaphore()
    for axis, n, me in (("ex", n_ex, ex), ("ft", n_ft, ft)):
        @pl.loop(1, n)
        def _(d):
            pl.semaphore_signal(
                barrier, inc=1, device_id={axis: lax.rem(me + d, n)}, device_id_type=MESH
            )
    pl.semaphore_wait(barrier, n_ex + n_ft - 2)

    groups = {}

    def send(name, axis, src, dst, region):
        n, me = {"ex": (n_ex, ex), "ft": (n_ft, ft), "in": (n_in, inner), "out": (n_out, outer)}[axis]
        g = len(groups)
        groups[name] = (g, region)

        @pl.loop(1, n)
        def _(d):
            peer = lax.rem(me + d, n)
            device = {
                "ex": {"ex": peer},
                "ft": {"ft": peer},
                "in": {"ft": outer * n_in + peer},
                "out": {"ft": peer * n_in + inner},
            }[axis]
            pltpu.make_async_remote_copy(
                src_ref=src(peer), dst_ref=dst, send_sem=ssem.at[g], recv_sem=rsem.at[g],
                device_id=device, device_id_type=MESH,
            ).start()

    def arrive(name):
        g, region = groups[name]
        pltpu.make_async_copy(region, region, rsem.at[g]).wait()

    def put_norm(k, axis, square):
        buf, n, me = (nx, n_ex, ex) if axis == "ex" else (nf, n_ft, ft)
        buf[k, me] = jnp.broadcast_to(square, (8, 128))
        own = buf.at[k, me]
        send(("norm", axis, k), axis, lambda peer: own, own, buf.at[k, pl.ds(0, n - 1)])

    def total_norm(k, axis):
        buf, n = (nx, n_ex) if axis == "ex" else (nf, n_ft)
        arrive(("norm", axis, k))
        total = buf[k, 0]
        for i in range(1, n):
            total = total + buf[k, i]
        return total[:, :1]

    def get_norm(k, axis):
        return jnp.sqrt(total_norm(k, axis) + eps)

    def spread(buf, name, j, value):
        buf[j, ex] = value
        own = buf.at[j, ex]
        send((name, j), "ex", lambda peer: own, own, buf.at[j, pl.ds(0, n_ex - 1)])

    def gathered(buf, name, j):
        arrive((name, j))
        total = buf[j, 0]
        for i in range(1, n_ex):
            total = total + buf[j, i]
        return total

    def times_rows(c, first, chunks=CHUNKS):
        @pl.loop(0, chunks)
        def _(i):
            r = pl.ds(pl.multiple_of(i * rc, rc), rc)
            out = lax.dot_general(w16[:, c], av[r, c], NT, preferred_element_type=F32)
            acc[:, r] = out if first else acc[:, r] + out

    def rows_send(q, ch, c, first):
        r = pl.ds(ch * rc, rc)
        out = lax.dot_general(w16[:, c], av[r, c], NT, preferred_element_type=F32)
        out = fold(out if first else acc[:, r] + out)
        for i in range(n_ft):
            qs[q, ch, i // n_out, i % n_out] = out[:, i * piece:(i + 1) * piece]
        r1[q, ch, inner] = qs[q, ch, inner]
        send(
            ("r1", q, ch), "in", lambda peer: qs.at[q, ch, peer], r1.at[q, ch, inner],
            r1.at[q, ch, pl.ds(0, n_in - 1)],
        )

    def inner_sum(q, ch):
        arrive(("r1", q, ch))
        total = r1[q, ch, 0]
        for i in range(1, n_in):
            total = total + r1[q, ch, i]
        s1[q, ch] = total
        r2[q, ch, outer] = s1[q, ch, outer]
        send(
            ("r2", q, ch), "out", lambda peer: s1.at[q, ch, peer], r2.at[q, ch, outer],
            r2.at[q, ch, pl.ds(0, n_out - 1)],
        )

    def outer_sum(q, ch):
        arrive(("r2", q, ch))
        total = r2[q, ch, 0]
        for i in range(1, n_out):
            total = total + r2[q, ch, i]
        ag[q, ch, inner, outer] = total
        return total

    def outer_gather(q, ch):
        own = ag.at[q, ch, inner, outer]
        send(
            ("g1", q, ch), "out", lambda peer: own, own,
            ag.at[q, ch, inner, pl.ds(0, n_out - 1)],
        )

    def inner_gather(q, ch):
        arrive(("g1", q, ch))
        own = ag.at[q, ch, inner]
        send(("g2", q, ch), "in", lambda peer: own, own, ag.at[q, ch, pl.ds(0, n_in - 1)])

    def rows_get(q, ch):
        arrive(("g2", q, ch))
        return jnp.concatenate([ag[q, ch, i // n_out, i % n_out] for i in range(n_ft)], axis=1)

    put_norm(0, "ex", squares(t_ref[...]))
    u16[...] = split16(t_ref[...])

    def first_columns(j):
        loads[j].wait()
        c = pl.ds(j * cb, cb)
        spread(p0, "p0", j, fold(jnp.dot(u16[...], av[:, c], preferred_element_type=F32)))

    first_columns(0)
    first_columns(1)
    beta0 = get_norm(0, "ex")
    left[...] = t_ref[...] / beta0
    square = jnp.zeros((8, 1), F32)
    for j in range(BLOCKS):
        c = pl.ds(j * cb, cb)
        fresh = gathered(p0, "p0", j) / beta0
        square = square + squares(fresh)
        rp[:, c] = fresh
        w16[:, c] = split16(fresh)
        if j == BLOCKS - 1:
            put_norm(0, "ft", square)
            break
        times_rows(c, j == 0, CHUNKS if j < BLOCKS - 2 else CHUNKS // 2)
        if j + 2 < BLOCKS:
            first_columns(j + 2)

    for ch in range(CHUNKS):
        late = ch >= CHUNKS // 2
        done = (BLOCKS - 2 if late else BLOCKS - 1) * cb
        rows_send(0, ch, pl.ds(done, cols - done), False)
        if ch >= 1:
            inner_sum(0, ch - 1)
        if ch >= 2:
            outer_sum(0, ch - 2)
            outer_gather(0, ch - 2)
        if ch >= 3:
            inner_gather(0, ch - 3)
    alpha0 = get_norm(0, "ft")

    square = jnp.zeros((8, 1), F32)
    for ch in range(CHUNKS):
        if ch + 3 < CHUNKS:
            inner_sum(0, ch + 3)
        if ch + 2 < CHUNKS:
            outer_sum(0, ch + 2)
            outer_gather(0, ch + 2)
        if ch + 1 < CHUNKS:
            inner_gather(0, ch + 1)
        r = pl.ds(ch * rc, rc)
        fresh = rows_get(0, ch) / alpha0 - alpha0 * left[:, r]
        square = square + squares(fresh)
        left[:, r] = fresh
        u16[:, r] = split16(fresh)
        if ch < CHUNKS - 1:
            out = jnp.dot(u16[:, r], av[r, :], preferred_element_type=F32)
            pacc[...] = out if ch == 0 else pacc[...] + out
        else:
            put_norm(1, "ex", square)
            for h in range(2):
                c = pl.ds(h * half, half)
                out = jnp.dot(u16[:, r], av[r, c], preferred_element_type=F32)
                spread(p1, "p1", h, fold(pacc[:, c] + out))
    beta1 = get_norm(1, "ex")

    square = jnp.zeros((8, 1), F32)
    for h in range(2):
        c = pl.ds(h * half, half)
        v0 = rp[:, c] / alpha0
        fresh = gathered(p1, "p1", h) / beta1 - beta1 * v0
        square = square + squares(fresh)
        rp[:, c] = v0
        est_ref[:, c] = fresh
        w16[:, c] = split16(fresh)
        if h == 0:
            times_rows(c, True, CHUNKS // 2)
    put_norm(1, "ft", square)
    def piece_square(ch, total):
        at = ch * rc + (inner * n_out + outer) * piece
        old = left[:, pl.ds(pl.multiple_of(at, piece), piece)]
        return squares(total / alpha1 - alpha1 * (old / beta1))

    square = jnp.zeros((8, 1), F32)
    alpha1 = None
    for ch in range(CHUNKS):
        late = ch >= CHUNKS // 2
        rows_send(1, ch, pl.ds(0, cols) if late else pl.ds(half, half), late)
        if ch >= 1:
            inner_sum(1, ch - 1)
        if ch >= 2:
            if alpha1 is None:
                alpha1 = get_norm(1, "ft")
            square = square + piece_square(ch - 2, outer_sum(1, ch - 2))
            outer_gather(1, ch - 2)
        if ch >= 3:
            inner_gather(1, ch - 3)
    inner_sum(1, CHUNKS - 1)
    square = square + piece_square(CHUNKS - 2, outer_sum(1, CHUNKS - 2))
    outer_gather(1, CHUNKS - 2)
    square = square + piece_square(CHUNKS - 1, outer_sum(1, CHUNKS - 1))
    put_norm(2, "ft", square)
    outer_gather(1, CHUNKS - 1)
    inner_gather(1, CHUNKS - 3)
    inner_gather(1, CHUNKS - 2)
    put_norm(2, "ex", total_norm(2, "ft"))
    inner_gather(1, CHUNKS - 1)
    beta2 = get_norm(2, "ex")

    rho = jnp.sqrt(alpha0 * alpha0 + beta1 * beta1)
    cosine = alpha0 / rho
    sine = beta1 / rho
    theta = sine * alpha1
    rho_bar = -cosine * alpha1
    step1 = cosine * beta0 / rho
    rho2 = jnp.sqrt(rho_bar * rho_bar + beta2 * beta2)
    step2 = rho_bar / rho2 * (sine * beta0) / rho2
    weight0 = step1 - step2 * (theta / rho)
    est_ref[...] = weight0 * rp[...] + step2 * (est_ref[...] / alpha1)
    scale0 = weight0 / alpha0
    scale1 = step2 / alpha1
    for ch in range(CHUNKS):
        arrive(("g2", 1, ch))
        for i in range(n_ft):
            r = pl.ds(ch * rc + i * piece, piece)
            at = (ch, i // n_out, i % n_out)
            mis_ref[:, r] = t_ref[:, r] - (scale0 * ag[(0, *at)] + scale1 * ag[(1, *at)])

    for g, region in groups.values():
        pltpu.make_async_copy(region, region, ssem.at[g]).wait()


def solution(mesh):
    n_ex, n_ft = mesh.shape["ex"], mesh.shape["ft"]
    n_in = 4 if n_ft % 16 == 0 else 2

    def shards(features, targets):
        rows, cols = features.shape
        piece = rows // CHUNKS // n_ft
        n_groups = BLOCKS + 2 + 8 * CHUNKS + 6
        vmem = pltpu.VMEM
        return pl.pallas_call(
            functools.partial(kernel, n_ex, n_ft, n_in),
            out_shape=(
                jax.ShapeDtypeStruct((8, cols), F32),
                jax.ShapeDtypeStruct((8, rows), F32),
            ),
            in_specs=[pl.BlockSpec(memory_space=pl.ANY), pl.BlockSpec(memory_space=vmem)],
            out_specs=(pl.BlockSpec(memory_space=vmem), pl.BlockSpec(memory_space=vmem)),
            scratch_shapes=[
                vmem((rows, cols), jnp.bfloat16),
                vmem((16, rows), jnp.bfloat16),
                vmem((16, cols), jnp.bfloat16),
                vmem((16, rows), F32),
                vmem((16, cols), F32),
                vmem((8, cols), F32),
                vmem((8, rows), F32),
                vmem((BLOCKS, n_ex, 8, cols // BLOCKS), F32),
                vmem((2, n_ex, 8, cols // 2), F32),
                vmem((2, CHUNKS, n_in, n_ft // n_in, 8, piece), F32),
                vmem((2, CHUNKS, n_in, n_ft // n_in, 8, piece), F32),
                vmem((2, CHUNKS, n_ft // n_in, 8, piece), F32),
                vmem((2, CHUNKS, n_ft // n_in, 8, piece), F32),
                vmem((2, CHUNKS, n_in, n_ft // n_in, 8, piece), F32),
                vmem((3, n_ex, 8, 128), F32),
                vmem((3, n_ft, 8, 128), F32),
                pltpu.SemaphoreType.DMA((BLOCKS,)),
                pltpu.SemaphoreType.DMA((n_groups,)),
                pltpu.SemaphoreType.DMA((n_groups,)),
            ],
            compiler_params=pltpu.CompilerParams(
                collective_id=0, has_side_effects=True, vmem_limit_bytes=58 << 20
            ),
        )(features, targets)

    return jax.shard_map(
        shards,
        mesh=mesh,
        in_specs=(P("ex", "ft"), P(None, "ex")),
        out_specs=(P(None, "ft"), P(None, "ex")),
        check_vma=False,
    )
```

```python
import functools

import jax
import jax.numpy as jnp
from jax import lax
from jax.experimental import pallas as pl
from jax.experimental.pallas import tpu as pltpu
from jax.sharding import PartitionSpec as P

eps = 1e-06
F32 = jnp.float32
MESH = pl.DeviceIdType.MESH
NT = (((1,), (1,)), ((), ()))

BLOCKS = 4
CHUNKS = 4


def split16(x):
    hi = x.astype(jnp.bfloat16).astype(F32)
    return jnp.concatenate([hi, x - hi], axis=0).astype(jnp.bfloat16)


def fold(r):
    return r[:8] + r[8:]


def squares(x):
    return jnp.sum(x * x, axis=1, keepdims=True)


def kernel(
    n_ex, n_ft, a_ref, t_ref, est_ref, mis_ref,
    av, u16, w16, acc, pacc, rp, left, p0, p1, qs, rsb, ag, nx, nf,
    hbm, ssem, rsem,
):
    rows, cols = av.shape
    cb = cols // BLOCKS
    rc = rows // CHUNKS
    piece = rc // n_ft
    half = cols // 2
    ex, ft = lax.axis_index("ex"), lax.axis_index("ft")

    loads = []
    for j in range(BLOCKS):
        c = pl.ds(j * cb, cb)
        load = pltpu.make_async_copy(a_ref.at[:, c], av.at[:, c], hbm.at[j])
        load.start()
        loads.append(load)

    barrier = pltpu.get_barrier_semaphore()
    for axis, n, me in (("ex", n_ex, ex), ("ft", n_ft, ft)):
        @pl.loop(1, n)
        def _(d):
            pl.semaphore_signal(
                barrier, inc=1, device_id={axis: lax.rem(me + d, n)}, device_id_type=MESH
            )
    pl.semaphore_wait(barrier, n_ex + n_ft - 2)

    groups = {}

    def send(name, axis, src, dst, region):
        n, me = (n_ex, ex) if axis == "ex" else (n_ft, ft)
        g = len(groups)
        groups[name] = (g, region)

        @pl.loop(1, n)
        def _(d):
            peer = lax.rem(me + d, n)
            pltpu.make_async_remote_copy(
                src_ref=src(peer), dst_ref=dst, send_sem=ssem.at[g], recv_sem=rsem.at[g],
                device_id={axis: peer}, device_id_type=MESH,
            ).start()

    def arrive(name):
        g, region = groups[name]
        pltpu.make_async_copy(region, region, rsem.at[g]).wait()

    def put_norm(k, axis, square):
        buf, n, me = (nx, n_ex, ex) if axis == "ex" else (nf, n_ft, ft)
        buf[k, me] = jnp.broadcast_to(square, (8, 128))
        own = buf.at[k, me]
        send(("norm", axis, k), axis, lambda peer: own, own, buf.at[k, pl.ds(0, n - 1)])

    def total_norm(k, axis):
        buf, n = (nx, n_ex) if axis == "ex" else (nf, n_ft)
        arrive(("norm", axis, k))
        total = buf[k, 0]
        for i in range(1, n):
            total = total + buf[k, i]
        return total[:, :1]

    def get_norm(k, axis):
        return jnp.sqrt(total_norm(k, axis) + eps)

    def spread(buf, name, j, value):
        buf[j, ex] = value
        own = buf.at[j, ex]
        send((name, j), "ex", lambda peer: own, own, buf.at[j, pl.ds(0, n_ex - 1)])

    def gathered(buf, name, j):
        arrive((name, j))
        total = buf[j, 0]
        for i in range(1, n_ex):
            total = total + buf[j, i]
        return total

    def times_rows(c, first, chunks=CHUNKS):
        @pl.loop(0, chunks)
        def _(i):
            r = pl.ds(pl.multiple_of(i * rc, rc), rc)
            out = lax.dot_general(w16[:, c], av[r, c], NT, preferred_element_type=F32)
            acc[:, r] = out if first else acc[:, r] + out

    def rows_send(q, ch, c, first):
        r = pl.ds(ch * rc, rc)
        out = lax.dot_general(w16[:, c], av[r, c], NT, preferred_element_type=F32)
        out = fold(out if first else acc[:, r] + out)
        for i in range(n_ft):
            qs[q, ch, i] = out[:, i * piece:(i + 1) * piece]
        rsb[q, ch, ft] = qs[q, ch, ft]
        send(
            ("rs", q, ch), "ft", lambda peer: qs.at[q, ch, peer], rsb.at[q, ch, ft],
            rsb.at[q, ch, pl.ds(0, n_ft - 1)],
        )

    def rows_sum(q, ch):
        arrive(("rs", q, ch))
        total = rsb[q, ch, 0]
        for i in range(1, n_ft):
            total = total + rsb[q, ch, i]
        ag[q, ch, ft] = total
        return total

    def rows_gather(q, ch):
        own = ag.at[q, ch, ft]
        send(("ag", q, ch), "ft", lambda peer: own, own, ag.at[q, ch, pl.ds(0, n_ft - 1)])

    def rows_get(q, ch):
        arrive(("ag", q, ch))
        return jnp.concatenate([ag[q, ch, i] for i in range(n_ft)], axis=1)

    put_norm(0, "ex", squares(t_ref[...]))
    u16[...] = split16(t_ref[...])

    def first_columns(j):
        loads[j].wait()
        c = pl.ds(j * cb, cb)
        spread(p0, "p0", j, fold(jnp.dot(u16[...], av[:, c], preferred_element_type=F32)))

    first_columns(0)
    first_columns(1)
    beta0 = get_norm(0, "ex")
    left[...] = t_ref[...] / beta0
    square = jnp.zeros((8, 1), F32)
    for j in range(BLOCKS):
        c = pl.ds(j * cb, cb)
        fresh = gathered(p0, "p0", j) / beta0
        square = square + squares(fresh)
        rp[:, c] = fresh
        w16[:, c] = split16(fresh)
        if j == BLOCKS - 1:
            put_norm(0, "ft", square)
            break
        times_rows(c, j == 0, CHUNKS if j < BLOCKS - 2 else CHUNKS // 2)
        if j + 2 < BLOCKS:
            first_columns(j + 2)

    for ch in range(CHUNKS):
        late = ch >= CHUNKS // 2
        done = (BLOCKS - 2 if late else BLOCKS - 1) * cb
        rows_send(0, ch, pl.ds(done, cols - done), False)
        if ch >= 2:
            rows_sum(0, ch - 2)
            rows_gather(0, ch - 2)
    alpha0 = get_norm(0, "ft")

    square = jnp.zeros((8, 1), F32)
    for ch in range(CHUNKS):
        if ch + 2 < CHUNKS:
            rows_sum(0, ch + 2)
            rows_gather(0, ch + 2)
        r = pl.ds(ch * rc, rc)
        fresh = rows_get(0, ch) / alpha0 - alpha0 * left[:, r]
        square = square + squares(fresh)
        left[:, r] = fresh
        u16[:, r] = split16(fresh)
        if ch < CHUNKS - 1:
            out = jnp.dot(u16[:, r], av[r, :], preferred_element_type=F32)
            pacc[...] = out if ch == 0 else pacc[...] + out
        else:
            put_norm(1, "ex", square)
            for h in range(2):
                c = pl.ds(h * half, half)
                out = jnp.dot(u16[:, r], av[r, c], preferred_element_type=F32)
                spread(p1, "p1", h, fold(pacc[:, c] + out))
    beta1 = get_norm(1, "ex")

    square = jnp.zeros((8, 1), F32)
    for h in range(2):
        c = pl.ds(h * half, half)
        v0 = rp[:, c] / alpha0
        fresh = gathered(p1, "p1", h) / beta1 - beta1 * v0
        square = square + squares(fresh)
        rp[:, c] = v0
        est_ref[:, c] = fresh
        w16[:, c] = split16(fresh)
        if h == 0:
            times_rows(c, True, CHUNKS // 2)
    put_norm(1, "ft", square)
    def piece_square(ch, total):
        at = ch * rc + ft * piece
        old = left[:, pl.ds(pl.multiple_of(at, piece), piece)]
        return squares(total / alpha1 - alpha1 * (old / beta1))

    square = jnp.zeros((8, 1), F32)
    alpha1 = None
    for ch in range(CHUNKS):
        late = ch >= CHUNKS // 2
        rows_send(1, ch, pl.ds(0, cols) if late else pl.ds(half, half), late)
        if ch >= 2:
            if alpha1 is None:
                alpha1 = get_norm(1, "ft")
            square = square + piece_square(ch - 2, rows_sum(1, ch - 2))
            rows_gather(1, ch - 2)
    square = square + piece_square(CHUNKS - 2, rows_sum(1, CHUNKS - 2))
    rows_gather(1, CHUNKS - 2)
    square = square + piece_square(CHUNKS - 1, rows_sum(1, CHUNKS - 1))
    put_norm(2, "ft", square)
    rows_gather(1, CHUNKS - 1)
    put_norm(2, "ex", total_norm(2, "ft"))
    beta2 = get_norm(2, "ex")

    rho = jnp.sqrt(alpha0 * alpha0 + beta1 * beta1)
    cosine = alpha0 / rho
    sine = beta1 / rho
    theta = sine * alpha1
    rho_bar = -cosine * alpha1
    step1 = cosine * beta0 / rho
    rho2 = jnp.sqrt(rho_bar * rho_bar + beta2 * beta2)
    step2 = rho_bar / rho2 * (sine * beta0) / rho2
    weight0 = step1 - step2 * (theta / rho)
    est_ref[...] = weight0 * rp[...] + step2 * (est_ref[...] / alpha1)
    scale0 = weight0 / alpha0
    scale1 = step2 / alpha1
    for ch in range(CHUNKS):
        arrive(("ag", 1, ch))
        for i in range(n_ft):
            r = pl.ds(ch * rc + i * piece, piece)
            mis_ref[:, r] = t_ref[:, r] - (scale0 * ag[0, ch, i] + scale1 * ag[1, ch, i])

    for g, region in groups.values():
        pltpu.make_async_copy(region, region, ssem.at[g]).wait()


def solution(mesh):
    n_ex, n_ft = mesh.shape["ex"], mesh.shape["ft"]

    def shards(features, targets):
        rows, cols = features.shape
        piece = rows // CHUNKS // n_ft
        n_groups = BLOCKS + 2 + 4 * CHUNKS + 6
        vmem = pltpu.VMEM
        return pl.pallas_call(
            functools.partial(kernel, n_ex, n_ft),
            out_shape=(
                jax.ShapeDtypeStruct((8, cols), F32),
                jax.ShapeDtypeStruct((8, rows), F32),
            ),
            in_specs=[pl.BlockSpec(memory_space=pl.ANY), pl.BlockSpec(memory_space=vmem)],
            out_specs=(pl.BlockSpec(memory_space=vmem), pl.BlockSpec(memory_space=vmem)),
            scratch_shapes=[
                vmem((rows, cols), jnp.bfloat16),
                vmem((16, rows), jnp.bfloat16),
                vmem((16, cols), jnp.bfloat16),
                vmem((16, rows), F32),
                vmem((16, cols), F32),
                vmem((8, cols), F32),
                vmem((8, rows), F32),
                vmem((BLOCKS, n_ex, 8, cols // BLOCKS), F32),
                vmem((2, n_ex, 8, cols // 2), F32),
                vmem((2, CHUNKS, n_ft, 8, piece), F32),
                vmem((2, CHUNKS, n_ft, 8, piece), F32),
                vmem((2, CHUNKS, n_ft, 8, piece), F32),
                vmem((3, n_ex, 8, 128), F32),
                vmem((3, n_ft, 8, 128), F32),
                pltpu.SemaphoreType.DMA((BLOCKS,)),
                pltpu.SemaphoreType.DMA((n_groups,)),
                pltpu.SemaphoreType.DMA((n_groups,)),
            ],
            compiler_params=pltpu.CompilerParams(
                collective_id=0, has_side_effects=True, vmem_limit_bytes=58 << 20
            ),
        )(features, targets)

    return jax.shard_map(
        shards,
        mesh=mesh,
        in_specs=(P("ex", "ft"), P(None, "ex")),
        out_specs=(P(None, "ft"), P(None, "ex")),
        check_vma=False,
    )
```
